512 devices in a mesh: train: 128 (over z, y, core), feat: 4 (over x).
Axes of the slice: x: 4, y: 8, z: 8, core: 2. Of those that a mesh axis runs over, the one named last changes fastest.
Arguments:
- train_feats: bfloat16 [262144, 2048], P('train', 'feat'), may hold values from -180 to 180, as said below
- test_feats: bfloat16 [512, 2048], P('feat'), may hold values from -180 to 180, as said below
Outputs:
- scores: bfloat16 [262144, 512], P('train', 'feat')
The draws below stay inside these ranges and needn't reach their ends.
Inputs may be any that keep to these rules, and one draw needn't show every extreme that they name: `train_feats`: each training example has its own scale. `test_feats`: each test example has its own scale.
All inputs are finite; a program needn't handle non-finite values.
Results may differ from the reference program's by a relative error of at most 0.0058.
Values may be sent and summed in bfloat16 or wider, within the bound.
No kernel may reach another device: no remote copies, remote signals or barrier semaphores. Data moves between devices by JAX's collectives and lax.ppermute only.
A program may use at most 64 MiB of HBM per device.

```python
import math
import jax
import jax.numpy as jnp
from jax import lax

P_SIZE = 2048
ROWS = 2048
ITERS = 2
TRAIN_ROWS = 262144
TEST = 512


segment_count = 8


def segment_tables(key):
    first, second = jax.random.split(jax.random.fold_in(key, 7))
    scales = jnp.exp(jax.random.uniform(first, (segment_count, P_SIZE), jnp.float32, 0.0, math.log(10.0)))
    signs = jnp.where(jax.random.bernoulli(second, 0.5, (segment_count, P_SIZE)), 1.0, -1.0).astype(jnp.float32)
    return (scales, signs)


def feature_block(key, count, row_lo, row_hi, scales, signs):
    groups = scales.shape[0]
    first, second, third = jax.random.split(key, 3)
    base = jnp.clip(jax.random.normal(first, (count, P_SIZE), jnp.float32), -3.0, 3.0)
    common = jnp.clip(jax.random.normal(second, (count, 16), jnp.float32), -3.0, 3.0)
    common = jnp.tile(common, (1, P_SIZE // 16))
    rows = jnp.exp(jax.random.uniform(third, (count, 1), jnp.float32, math.log(row_lo), math.log(row_hi)))
    base = base.reshape(groups, count // groups, P_SIZE)
    common = common.reshape(groups, count // groups, P_SIZE) * signs[:, None, :]
    rows = rows.reshape(groups, count // groups, 1)
    values = rows * scales[:, None, :] * (base + common)
    return values.reshape(count, P_SIZE).astype(jnp.bfloat16)


def draw_train_feats(key, part):
    scales, signs = segment_tables(key)
    key = jax.random.fold_in(key, 1)
    return feature_block(key, TRAIN_ROWS, 0.3, 3.0, scales, signs)


def draw_test_feats(key, part):
    scales, signs = segment_tables(key)
    key = jax.random.fold_in(key, 2)
    return feature_block(key, TEST, 0.5, 2.0, scales[0:1], signs[0:1])


def setup_inputs(seed: int = 0) -> dict:
    arg_keys = jax.random.split(jax.random.key(seed), 3)
    train_feats = draw_train_feats(jax.random.fold_in(arg_keys[2], 71), 0)
    test_feats = draw_test_feats(jax.random.fold_in(arg_keys[2], 71), 0)
    return {"train_feats": train_feats, "test_feats": test_feats}


damping = 0.05

def reference(train_feats, test_feats):
    total_rows = train_feats.shape[0]
    width = train_feats.shape[1]
    blocks = train_feats.reshape(-1, ROWS, width)
    energy = lax.map(lambda blk: lax.optimization_barrier(jnp.sum(jnp.square(blk.astype(jnp.float32)), axis=0)), blocks)
    diag = lax.optimization_barrier(jnp.sum(energy, axis=0))[:, None] / total_rows + damping
    rhs = test_feats.astype(jnp.float32).T

    def operate(direction):
        prod = jnp.dot(train_feats, direction.astype(jnp.bfloat16), preferred_element_type=jnp.float32)
        back = jnp.dot(train_feats.T, prod.astype(jnp.bfloat16), preferred_element_type=jnp.float32)
        return back / total_rows + damping * direction
    solution = jnp.zeros_like(rhs)
    resid = rhs
    precond = resid / diag
    search = precond
    rz_now = lax.optimization_barrier(jnp.sum(resid * precond, axis=0))
    for step in range(ITERS):
        image = operate(search)
        alpha = rz_now / lax.optimization_barrier(jnp.sum(search * image, axis=0))
        solution = solution + alpha * search
        resid = resid - alpha * image
        precond = resid / diag
        rz_next = lax.optimization_barrier(jnp.sum(resid * precond, axis=0))
        search = precond + rz_next / rz_now * search
        rz_now = rz_next
    out = jnp.dot(train_feats, solution.astype(jnp.bfloat16), preferred_element_type=jnp.float32)
    return (out * (1.0 / jnp.sqrt(jnp.float32(width)))).astype(jnp.bfloat16)
```

```python
import jax
import jax.numpy as jnp
from jax import lax
from jax.sharding import PartitionSpec as P

damping = 0.05
bf16 = jnp.bfloat16
f32 = jnp.float32


def ring(size, step):
    return [(i, (i + step) % size) for i in range(size)]


def everyone(value, axis, count):
    return lax.all_to_all(jnp.broadcast_to(value[None], (count,) + value.shape), axis, 0, 0, tiled=True)


def split3(value):
    first = lax.reduce_precision(value, 8, 7)
    second = lax.reduce_precision(value - first, 8, 7)
    third = value - first - second
    return first.astype(bf16), second.astype(bf16), third.astype(bf16)


def local(train_feats, test_feats):
    rows, block = train_feats.shape
    tests, width = test_feats.shape
    feats = lax.axis_size("feat")
    members = lax.axis_size("train")
    total_rows = rows * members
    half = rows // 2
    me = lax.axis_index("feat")
    owner = lax.axis_index("train")
    right, left = ring(feats, 1), ring(feats, -1)

    low, high = train_feats[:half], train_feats[half:]
    prev_low = lax.ppermute(low, "feat", right)
    next_high = lax.ppermute(high, "feat", left)
    prev_high = lax.ppermute(high, "feat", right)
    next_low = lax.ppermute(low, "feat", left)
    far_low = lax.ppermute(prev_low, "feat", right)
    far_high = lax.ppermute(next_high, "feat", left)

    order = [me, (me + feats - 1) % feats, (me + 1) % feats, (me + 2) % feats]
    energy = jnp.sum(jnp.square(train_feats.astype(f32)), axis=0).reshape(block // 128, 128)
    energy = jnp.sum(everyone(energy, "train", members), axis=0)
    energy = everyone(energy, "feat", feats)
    diag = jnp.concatenate([lax.dynamic_index_in_dim(energy, o, 0, False) for o in order], 0)
    diag = diag / total_rows + damping
    rhs = jnp.concatenate([lax.dynamic_slice_in_dim(test_feats, o * block, block, 1) for o in order], 1)
    rhs = rhs.astype(f32)
    search0 = rhs / diag.reshape(1, width)
    dir0 = search0.astype(bf16).T

    halves = [
        (low, prev_low, next_low, far_low),
        (high, prev_high, next_high, far_high),
    ]

    def forward(direction):
        out = []
        for parts in halves:
            total = 0.0
            for i, part in enumerate(parts):
                total = total + jnp.dot(part, direction[i * block:(i + 1) * block], preferred_element_type=f32)
            out.append(total)
        return out

    prod = [p.astype(bf16) for p in forward(dir0)]
    back = [
        sum(
            jnp.einsum("nm,np->mp", prod[h], halves[h][i], preferred_element_type=f32)
            for h in range(2)
        )
        for i in range(4)
    ]
    back = jnp.concatenate(back, 1).astype(bf16).reshape(tests, width // 128, 128)
    back = lax.all_to_all(back, "train", 0, 0, tiled=True)
    back = jnp.sum(back.astype(f32), axis=0)

    mine = lax.dynamic_index_in_dim(rhs, owner, 0, False).reshape(width // 128, 128)
    precond = mine / diag
    rz0 = jnp.sum(mine * precond)
    image = back / total_rows + damping * precond
    alpha0 = rz0 / jnp.sum(precond * image)
    resid = mine - alpha0 * image
    precond1 = resid / diag
    rz1 = jnp.sum(resid * precond1)
    search1 = precond1 + rz1 / rz0 * precond
    norm1 = jnp.sum(search1 * search1)
    scalars = jnp.stack([jnp.stack(split3(s)) for s in (alpha0, rz1, norm1)]).reshape(9)
    extra = jnp.zeros((8, 128), bf16).at[0, :9].set(scalars)
    message = jnp.concatenate([search1.astype(bf16), extra], 0)
    message = everyone(message, "train", members)
    dir1t = message[:, : width // 128].reshape(tests, width)
    dir1 = dir1t.T
    pieces = message[:, width // 128, :9].astype(f32).reshape(tests, 3, 3)
    alpha0, rz1, norm1 = jnp.sum(pieces, axis=2).T

    prod1 = forward(dir1)
    square = sum(jnp.sum(p * p, axis=0) for p in prod1)
    square = jnp.sum(everyone(square.reshape(1, tests), "train", members), axis=(0, 1))
    alpha1 = rz1 / (square / total_rows + damping * norm1)
    answer = alpha0[:, None] * search0 + alpha1[:, None] * dir1t.astype(f32)
    out = forward(answer.astype(bf16).T)
    scale = 1.0 / jnp.sqrt(f32(width))
    return jnp.concatenate([(o * scale).astype(bf16) for o in out], 0)


def solution(mesh):
    return jax.shard_map(
        local,
        mesh=mesh,
        in_specs=(P("train", "feat"), P("feat", None)),
        out_specs=P("train", "feat"),
        check_vma=False,
    )
```

```python
import functools

import jax
import jax.numpy as jnp
from jax import lax
from jax.experimental import pallas as pl
from jax.experimental.pallas import tpu as pltpu
from jax.sharding import PartitionSpec as P

damping = 0.05
bf16 = jnp.bfloat16
f32 = jnp.float32
LANES = 128
TILE = 256
VMEM_BYTES = 20 * 1024 * 1024


def ring(size, step):
    return [(i, (i + step) % size) for i in range(size)]


def everyone(value, axis, count):
    return lax.all_to_all(jnp.broadcast_to(value[None], (count,) + value.shape), axis, 0, 0, tiled=True)


def times(parts, direction_ref):
    total = None
    for i, part in enumerate(parts):
        block = part.shape[1]
        term = jnp.dot(part[...], direction_ref[i * block:(i + 1) * block, :], preferred_element_type=f32)
        total = term if total is None else total + term
    return total


def first_kernel(*refs):
    low, high = refs[0:4], refs[4:8]
    direction, back, prod_low, prod_high, norm, total, spread = refs[8:]
    step = pl.program_id(0)

    @pl.when(step == 0)
    def _():
        total[...] = jnp.zeros_like(total)
        norm[...] = jnp.zeros_like(norm)

    block = low[0].shape[1]
    for parts, prod in ((low, prod_low), (high, prod_high)):
        value = times(parts, direction)
        prod[...] = value
        norm[...] += jnp.sum(value * value, axis=0, keepdims=True)
        turned = value.T.astype(bf16)
        for i, part in enumerate(parts):
            total[:, i * block:(i + 1) * block] += jnp.dot(turned, part[...], preferred_element_type=f32)

    @pl.when(step == pl.num_programs(0) - 1)
    def _():
        count = total.shape[1] // LANES
        tests = total.shape[0]
        for j in range(count):
            spread[pl.ds(j, tests, stride=count), :] = total[:, j * LANES:(j + 1) * LANES]
        back[...] = spread[...].astype(bf16)


def first(low, high, direction):
    rows, block = low[0].shape
    width, tests = direction.shape
    tile = pl.BlockSpec((TILE, block), lambda i: (i, 0))
    out = pl.BlockSpec((TILE, tests), lambda i: (i, 0))
    whole = lambda *shape: pl.BlockSpec(shape, lambda i: (0, 0))
    count = width // LANES
    return pl.pallas_call(
        first_kernel,
        grid=(rows // TILE,),
        in_specs=[tile] * 8 + [whole(width, tests)],
        out_specs=[whole(tests * count, LANES), out, out, whole(1, tests)],
        out_shape=[
            jax.ShapeDtypeStruct((tests * count, LANES), bf16),
            jax.ShapeDtypeStruct((rows, tests), f32),
            jax.ShapeDtypeStruct((rows, tests), f32),
            jax.ShapeDtypeStruct((1, tests), f32),
        ],
        scratch_shapes=[pltpu.VMEM((tests, width), f32), pltpu.VMEM((tests * count, LANES), f32)],
        compiler_params=pltpu.CompilerParams(vmem_limit_bytes=VMEM_BYTES),
        cost_estimate=pl.CostEstimate(flops=8 * rows * width * tests, bytes_accessed=4 * rows * width, transcendentals=0),
        name="first",
    )(*low, *high, direction)


def column_kernel(total_rows, parts, diag_ref, mine_ref, out):
    diag, mine = diag_ref[...], mine_ref[...]

    def dot(a, b):
        return jnp.sum(jnp.sum(a * b, axis=0, keepdims=True), axis=1, keepdims=True)

    back = jnp.sum(parts[...].astype(f32), axis=0)
    precond = mine / diag
    rz0 = dot(mine, precond)
    image = back / total_rows + damping * precond
    alpha0 = rz0 / dot(precond, image)
    resid = mine - alpha0 * image
    precond1 = resid / diag
    search = precond1 + dot(resid, precond1) / rz0 * precond
    out[...] = jnp.broadcast_to(search.astype(bf16)[None], out.shape)


def column(total_rows, parts, diag, mine):
    return pl.pallas_call(
        functools.partial(column_kernel, total_rows),
        out_shape=jax.ShapeDtypeStruct(parts.shape, bf16),
        compiler_params=pltpu.CompilerParams(vmem_limit_bytes=VMEM_BYTES),
        name="column",
    )(parts, diag, mine)


def second_kernel(*refs):
    low, high = refs[0:4], refs[4:8]
    message, rhs, prod_low, prod_high, stats, wide, direction = refs[8:]
    step = pl.program_id(0)

    @pl.when(step == 0)
    def _():
        count = rhs.shape[1] // LANES
        tests = rhs.shape[0]
        wide[...] = message[...].astype(f32)
        along = jnp.zeros((LANES, tests), f32)
        norm = jnp.zeros((LANES, tests), f32)
        for j in range(count):
            piece = wide[pl.ds(j, tests, stride=count), :].T
            along += piece * rhs[:, j * LANES:(j + 1) * LANES].astype(f32).T
            norm += piece * piece
            direction[j * LANES:(j + 1) * LANES, :] = piece.astype(bf16)
        stats[...] = jnp.zeros_like(stats)
        stats[1:2, :] = jnp.sum(along, axis=0, keepdims=True)
        stats[2:3, :] = jnp.sum(norm, axis=0, keepdims=True)

    for parts, prod in ((low, prod_low), (high, prod_high)):
        value = times(parts, direction)
        prod[...] = value
        stats[0:1, :] += jnp.sum(value * value, axis=0, keepdims=True)


def second(low, high, message, rhs):
    rows, block = low[0].shape
    tests, width = rhs.shape
    tile = pl.BlockSpec((TILE, block), lambda i: (i, 0))
    out = pl.BlockSpec((TILE, tests), lambda i: (i, 0))
    whole = lambda *shape: pl.BlockSpec(shape, lambda i: (0, 0))
    return pl.pallas_call(
        second_kernel,
        grid=(rows // TILE,),
        in_specs=[tile] * 8 + [whole(*message.shape), whole(tests, width)],
        out_specs=[out, out, whole(8, tests)],
        out_shape=[
            jax.ShapeDtypeStruct((rows, tests), f32),
            jax.ShapeDtypeStruct((rows, tests), f32),
            jax.ShapeDtypeStruct((8, tests), f32),
        ],
        scratch_shapes=[pltpu.VMEM(message.shape, f32), pltpu.VMEM((width, tests), bf16)],
        compiler_params=pltpu.CompilerParams(vmem_limit_bytes=VMEM_BYTES),
        cost_estimate=pl.CostEstimate(flops=4 * rows * width * tests, bytes_accessed=4 * rows * width, transcendentals=0),
        name="second",
    )(*low, *high, message, rhs)


def last_kernel(total_rows, scale, norms, start, stats, a_low, a_high, b_low, b_high, out):
    members = norms.shape[0] // 2
    norm0 = jnp.sum(norms[pl.ds(0, members, stride=2), :], axis=0, keepdims=True)
    norm1 = jnp.sum(norms[pl.ds(1, members, stride=2), :], axis=0, keepdims=True)
    alpha0 = start[0:1, :] / (norm0 / total_rows + damping * start[1:2, :])
    alpha1 = stats[1:2, :] / (norm1 / total_rows + damping * stats[2:3, :])
    alpha0, alpha1 = alpha0 * scale, alpha1 * scale
    half = a_low.shape[0]
    out[0:half, :] = (alpha0 * a_low[...] + alpha1 * b_low[...]).astype(bf16)
    out[half:, :] = (alpha0 * a_high[...] + alpha1 * b_high[...]).astype(bf16)


def last(total_rows, scale, norms, start, stats, prod0, prod1):
    half, tests = prod0[0].shape
    return pl.pallas_call(
        functools.partial(last_kernel, total_rows, scale),
        out_shape=jax.ShapeDtypeStruct((2 * half, tests), bf16),
        compiler_params=pltpu.CompilerParams(vmem_limit_bytes=VMEM_BYTES),
        name="last",
    )(norms, start, stats, *prod0, *prod1)


def local(train_feats, test_feats):
    rows, block = train_feats.shape
    tests, width = test_feats.shape
    feats = lax.axis_size("feat")
    members = lax.axis_size("train")
    total_rows = rows * members
    half = rows // 2
    count = width // LANES
    me = lax.axis_index("feat")
    owner = lax.axis_index("train")
    right, left = ring(feats, 1), ring(feats, -1)

    low, high = lax.optimization_barrier((train_feats[:half], train_feats[half:]))
    prev_low = lax.ppermute(low, "feat", right)
    next_high = lax.ppermute(high, "feat", left)
    prev_high = lax.ppermute(high, "feat", right)
    next_low = lax.ppermute(low, "feat", left)

    order = [me, (me + feats - 1) % feats, (me + 1) % feats, (me + 2) % feats]
    energy = jnp.sum(jnp.square(low.astype(f32)), axis=0) + jnp.sum(jnp.square(high.astype(f32)), axis=0)
    energy = jnp.sum(everyone(energy.reshape(block // LANES, LANES), "train", members), axis=0)
    energy, prev_low, next_high = lax.optimization_barrier((energy, prev_low, next_high))
    far_low = lax.ppermute(prev_low, "feat", right)
    far_high = lax.ppermute(next_high, "feat", left)
    energy = everyone(energy, "feat", feats)
    diag = jnp.concatenate([lax.dynamic_index_in_dim(energy, o, 0, False) for o in order], 0)
    diag = diag / total_rows + damping
    rhs = jnp.concatenate([lax.dynamic_slice_in_dim(test_feats, o * block, block, 1) for o in order], 1)
    wide = rhs.astype(f32)
    search = wide / diag.reshape(1, width)
    start = jnp.stack([jnp.sum(wide * search, axis=1), jnp.sum(search * search, axis=1)])
    direction = search.astype(bf16).T
    mine = lax.dynamic_index_in_dim(rhs, owner, 0, False).astype(f32).reshape(count, LANES)

    lows = (low, prev_low, next_low, far_low)
    highs = (high, prev_high, next_high, far_high)
    back, *prod0, norm0 = first(lows, highs, direction)
    back = lax.all_to_all(back.reshape(tests, count, LANES), "train", 0, 0, tiled=True)
    message = column(total_rows, back, diag, mine)
    message = lax.all_to_all(message, "train", 0, 0, tiled=True)
    *prod1, stats = second(lows, highs, message.reshape(tests * count, LANES), rhs)
    norms = everyone(jnp.concatenate([norm0, stats[0:1]], 0), "train", members)
    scale = 1.0 / float(width) ** 0.5
    return last(total_rows, scale, norms.reshape(2 * members, tests), start, stats, prod0, prod1)


def solution(mesh):
    return jax.shard_map(
        local,
        mesh=mesh,
        in_specs=(P("train", "feat"), P("feat", None)),
        out_specs=P("train", "feat"),
        check_vma=False,
    )
```

```python
import functools

import jax
import jax.numpy as jnp
from jax import lax
from jax.experimental import pallas as pl
from jax.experimental.pallas import tpu as pltpu
from jax.sharding import PartitionSpec as P

damping = 0.05
bf16 = jnp.bfloat16
f32 = jnp.float32
LANES = 128
TILE = 256
EARLY = 768
VMEM_BYTES = 20 * 1024 * 1024


def ring(size, step):
    return [(i, (i + step) % size) for i in range(size)]


def everyone(value, axis, count):
    return lax.all_to_all(jnp.broadcast_to(value[None], (count,) + value.shape), axis, 0, 0, tiled=True)


def times(parts, direction_ref):
    total = None
    for i, part in enumerate(parts):
        block = part.shape[1]
        term = jnp.dot(part[...], direction_ref[i * block:(i + 1) * block, :], preferred_element_type=f32)
        total = term if total is None else total + term
    return total


def partial_kernel(*refs):
    low, high = refs[0:3], refs[3:6]
    direction, out_low, out_high = refs[6:]
    out_low[...] = times(low, direction)
    out_high[...] = times(high, direction)


def partial(low, high, direction):
    rows, block = low[0].shape
    width, tests = direction.shape
    tile = pl.BlockSpec((TILE, block), lambda i: (i, 0))
    out = pl.BlockSpec((TILE, tests), lambda i: (i, 0))
    return pl.pallas_call(
        partial_kernel,
        grid=(rows // TILE,),
        in_specs=[tile] * 6 + [pl.BlockSpec((width, tests), lambda i: (0, 0))],
        out_specs=[out, out],
        out_shape=[jax.ShapeDtypeStruct((rows, tests), f32)] * 2,
        compiler_params=pltpu.CompilerParams(vmem_limit_bytes=VMEM_BYTES),
        cost_estimate=pl.CostEstimate(flops=3 * rows * width * tests, bytes_accessed=3 * rows * width, transcendentals=0),
        name="partial",
    )(*low, *high, direction)


def first_kernel(final, *refs):
    low, high = refs[0:4], refs[4:8]
    direction, part_low, part_high, total_in, norm_in = refs[8:13]
    if final:
        back, norm, prod_low, prod_high, total, spread = refs[13:]
    else:
        total, norm, prod_low, prod_high = refs[13:]
    step = pl.program_id(0)

    @pl.when(step == 0)
    def _():
        total[...] = total_in[...]
        norm[...] = norm_in[...]

    block = low[0].shape[1]
    for parts, part, prod in ((low, part_low, prod_low), (high, part_high, prod_high)):
        value = part[...] + jnp.dot(parts[3][...], direction[3 * block:, :], preferred_element_type=f32)
        prod[...] = value
        norm[...] += jnp.sum(value * value, axis=0, keepdims=True)
        turned = value.T.astype(bf16)
        for i, tile in enumerate(parts):
            total[:, i * block:(i + 1) * block] += jnp.dot(turned, tile[...], preferred_element_type=f32)

    if final:
        @pl.when(step == pl.num_programs(0) - 1)
        def _():
            count = total.shape[1] // LANES
            tests = total.shape[0]
            for j in range(count):
                spread[pl.ds(j, tests, stride=count), :] = total[:, j * LANES:(j + 1) * LANES]
            back[...] = spread[...].astype(bf16)


def first(final, low, high, direction, part, total, norm, base):
    rows, block = low[3].shape
    width, tests = direction.shape
    skip = base // TILE
    shifted = pl.BlockSpec((TILE, block), lambda i: (i + skip, 0))
    own = pl.BlockSpec((TILE, block), lambda i: (i, 0))
    taken = pl.BlockSpec((TILE, tests), lambda i: (i + skip, 0))
    out = pl.BlockSpec((TILE, tests), lambda i: (i, 0))
    whole = lambda *shape: pl.BlockSpec(shape, lambda i: (0, 0))
    count = width // LANES
    sums = (tests * count, LANES) if final else (tests, width)
    return pl.pallas_call(
        functools.partial(first_kernel, final),
        grid=(rows // TILE,),
        in_specs=[shifted, shifted, shifted, own] * 2 + [whole(width, tests), taken, taken, whole(tests, width), whole(1, tests)],
        out_specs=[whole(*sums), whole(1, tests), out, out],
        out_shape=[
            jax.ShapeDtypeStruct(sums, bf16 if final else f32),
            jax.ShapeDtypeStruct((1, tests), f32),
            jax.ShapeDtypeStruct((rows, tests), f32),
            jax.ShapeDtypeStruct((rows, tests), f32),
        ],
        scratch_shapes=[pltpu.VMEM((tests, width), f32), pltpu.VMEM((tests * count, LANES), f32)] if final else [],
        compiler_params=pltpu.CompilerParams(vmem_limit_bytes=VMEM_BYTES),
        cost_estimate=pl.CostEstimate(flops=5 * rows * width * tests, bytes_accessed=4 * rows * width, transcendentals=0),
        name="first",
    )(*low, *high, direction, *part, total, norm)


def column_kernel(total_rows, parts, diag_ref, mine_ref, out):
    diag, mine = diag_ref[...], mine_ref[...]

    def dot(a, b):
        return jnp.sum(jnp.sum(a * b, axis=0, keepdims=True), axis=1, keepdims=True)

    back = jnp.sum(parts[...].astype(f32), axis=0)
    precond = mine / diag
    rz0 = dot(mine, precond)
    image = back / total_rows + damping * precond
    alpha0 = rz0 / dot(precond, image)
    resid = mine - alpha0 * image
    precond1 = resid / diag
    search = precond1 + dot(resid, precond1) / rz0 * precond
    out[...] = jnp.broadcast_to(search.astype(bf16)[None], out.shape)


def column(total_rows, parts, diag, mine):
    return pl.pallas_call(
        functools.partial(column_kernel, total_rows),
        out_shape=jax.ShapeDtypeStruct(parts.shape, bf16),
        compiler_params=pltpu.CompilerParams(vmem_limit_bytes=VMEM_BYTES),
        name="column",
    )(parts, diag, mine)


def second_kernel(early, *refs):
    low, high = refs[0:3], refs[3:6]
    far = refs[6:10]
    message, rhs, norm0, prod_low, prod_high, stats, norms, wide, direction, norm1 = refs[10:]
    step = pl.program_id(0)
    block = low[0].shape[1]

    @pl.when(step == 0)
    def _():
        count = rhs.shape[1] // LANES
        tests = rhs.shape[0]
        wide[...] = message[...].astype(f32)
        along = jnp.zeros((LANES, tests), f32)
        norm = jnp.zeros((LANES, tests), f32)
        for j in range(count):
            piece = wide[pl.ds(j, tests, stride=count), :]
            along += piece * rhs[:, j * LANES:(j + 1) * LANES].astype(f32)
            norm += piece * piece
            direction[j * LANES:(j + 1) * LANES, :] = piece.T.astype(bf16)
        norm1[...] = jnp.zeros_like(norm1)
        stats[...] = jnp.zeros_like(stats)
        stats[0:1, :] = jnp.sum(along.T, axis=0, keepdims=True)
        stats[1:2, :] = jnp.sum(norm.T, axis=0, keepdims=True)

    for parts, one, two, prod in ((low, far[0], far[1], prod_low), (high, far[2], far[3], prod_high)):
        last = jnp.where(step < early, one[...], two[...])
        value = times(parts, direction) + jnp.dot(last, direction[3 * block:, :], preferred_element_type=f32)
        prod[...] = value
        norm1[...] += jnp.sum(value * value, axis=0, keepdims=True)

    @pl.when(step == pl.num_programs(0) - 1)
    def _():
        even = lax.broadcasted_iota(jnp.int32, norms.shape, 0) % 2 == 0
        norms[...] = jnp.where(even, norm0[...], norm1[...])


def second(low, high, far, message, rhs, norm0, members):
    rows, block = low[0].shape
    tests, width = rhs.shape
    early, late = far[0].shape[0] // TILE, far[1].shape[0] // TILE
    tile = pl.BlockSpec((TILE, block), lambda i: (i, 0))
    one = pl.BlockSpec((TILE, block), lambda i: (jnp.minimum(i, early - 1), 0))
    two = pl.BlockSpec((TILE, block), lambda i: (jnp.maximum(i - early, 0), 0))
    out = pl.BlockSpec((TILE, tests), lambda i: (i, 0))
    whole = lambda *shape: pl.BlockSpec(shape, lambda i: (0, 0))
    return pl.pallas_call(
        functools.partial(second_kernel, early),
        grid=(early + late,),
        in_specs=[tile] * 6 + [one, two, one, two] + [whole(*message.shape), whole(tests, width), whole(1, tests)],
        out_specs=[out, out, whole(8, tests), whole(2 * members, tests)],
        out_shape=[
            jax.ShapeDtypeStruct((rows, tests), f32),
            jax.ShapeDtypeStruct((rows, tests), f32),
            jax.ShapeDtypeStruct((8, tests), f32),
            jax.ShapeDtypeStruct((2 * members, tests), f32),
        ],
        scratch_shapes=[pltpu.VMEM(message.shape, f32), pltpu.VMEM((width, tests), bf16), pltpu.VMEM((1, tests), f32)],
        compiler_params=pltpu.CompilerParams(vmem_limit_bytes=VMEM_BYTES),
        cost_estimate=pl.CostEstimate(flops=4 * rows * width * tests, bytes_accessed=4 * rows * width, transcendentals=0),
        name="second",
    )(*low, *high, *far, message, rhs, norm0)


def last_kernel(total_rows, scale, early, norms, start, stats, *refs):
    a_low, a_high, b_low, b_high, c_low, c_high, out = refs
    members = norms.shape[0] // 2
    norm0 = jnp.sum(norms[pl.ds(0, members, stride=2), :], axis=0, keepdims=True)
    norm1 = jnp.sum(norms[pl.ds(1, members, stride=2), :], axis=0, keepdims=True)
    alpha0 = start[0:1, :] / (norm0 / total_rows + damping * start[1:2, :])
    alpha1 = stats[0:1, :] / (norm1 / total_rows + damping * stats[1:2, :])
    alpha0, alpha1 = alpha0 * scale, alpha1 * scale
    half = c_low.shape[0]
    for base, one, two, both in ((0, a_low, b_low, c_low), (half, a_high, b_high, c_high)):
        out[base:base + early, :] = (alpha0 * one[...] + alpha1 * both[0:early, :]).astype(bf16)
        out[base + early:base + half, :] = (alpha0 * two[...] + alpha1 * both[early:, :]).astype(bf16)


def last(total_rows, scale, norms, start, stats, early, late, prod1):
    half, tests = prod1[0].shape
    return pl.pallas_call(
        functools.partial(last_kernel, total_rows, scale, early[0].shape[0]),
        out_shape=jax.ShapeDtypeStruct((2 * half, tests), bf16),
        compiler_params=pltpu.CompilerParams(vmem_limit_bytes=VMEM_BYTES),
        name="last",
    )(norms, start, stats, *early, *late, *prod1)


def local(train_feats, test_feats):
    rows, block = train_feats.shape
    tests, width = test_feats.shape
    feats = lax.axis_size("feat")
    members = lax.axis_size("train")
    total_rows = rows * members
    half = rows // 2
    count = width // LANES
    me = lax.axis_index("feat")
    owner = lax.axis_index("train")
    right, left = ring(feats, 1), ring(feats, -1)

    low, high = lax.optimization_barrier((train_feats[:half], train_feats[half:]))
    prev_low = lax.ppermute(low, "feat", right)
    next_high = lax.ppermute(high, "feat", left)
    prev_high = lax.ppermute(high, "feat", right)
    next_low = lax.ppermute(low, "feat", left)

    order = [me, (me + feats - 1) % feats, (me + 1) % feats, (me + 2) % feats]
    energy = jnp.sum(jnp.square(low.astype(f32)), axis=0) + jnp.sum(jnp.square(high.astype(f32)), axis=0)
    energy = jnp.sum(everyone(energy.reshape(block // LANES, LANES), "train", members), axis=0)
    energy, prev_low, next_high = lax.optimization_barrier((energy, prev_low, next_high))
    far_low = lax.ppermute(prev_low[:EARLY], "feat", right)
    far_high = lax.ppermute(next_high[:EARLY], "feat", left)
    far_low2 = lax.ppermute(prev_low[EARLY:], "feat", right)
    far_high2 = lax.ppermute(next_high[EARLY:], "feat", left)
    energy = everyone(energy, "feat", feats)
    diag = jnp.concatenate([lax.dynamic_index_in_dim(energy, o, 0, False) for o in order], 0)
    diag = diag / total_rows + damping
    rhs = jnp.concatenate([lax.dynamic_slice_in_dim(test_feats, o * block, block, 1) for o in order], 1)
    wide = rhs.astype(f32)
    search = wide / diag.reshape(1, width)
    start = jnp.stack([jnp.sum(wide * search, axis=1), jnp.sum(search * search, axis=1)])
    direction = search.astype(bf16).T
    mine = lax.dynamic_index_in_dim(rhs, owner, 0, False).astype(f32).reshape(count, LANES)

    lows, highs = (low, prev_low, next_low), (high, prev_high, next_high)
    part = partial(lows, highs, direction)
    zeros = jnp.zeros((tests, width), f32), jnp.zeros((1, tests), f32)
    total, norm0, *early = first(False, (*lows, far_low), (*highs, far_high), direction, part, *zeros, 0)
    total, mine, start = lax.optimization_barrier((total, mine, start))
    back, norm0, *late = first(True, (*lows, far_low2), (*highs, far_high2), direction, part, total, norm0, EARLY)
    back = lax.all_to_all(back.reshape(tests, count, LANES), "train", 0, 0, tiled=True)
    message = column(total_rows, back, diag, mine)
    message = lax.all_to_all(message, "train", 0, 0, tiled=True)
    far = (far_low, far_low2, far_high, far_high2)
    *prod1, stats, norms = second(lows, highs, far, message.reshape(tests * count, LANES), rhs, norm0, members)
    norms = lax.all_to_all(norms.reshape(members, 2, tests), "train", 0, 0, tiled=True)
    scale = 1.0 / float(width) ** 0.5
    return last(total_rows, scale, norms.reshape(2 * members, tests), start, stats, early, late, prod1)


def solution(mesh):
    return jax.shard_map(
        local,
        mesh=mesh,
        in_specs=(P("train", "feat"), P("feat", None)),
        out_specs=P("train", "feat"),
        check_vma=False,
    )
```
